32 devices in a mesh: groups: 2 (over y), gx: 4 (over z), col: 2 (over core), gy: 2 (over x).
Axes of the slice: x: 2, y: 2, z: 4, core: 2. Of those that a mesh axis runs over, the one named last changes fastest.
Arguments:
- volume: float32 [16, 32, 128, 256], P(('groups', 'gx'), 'gy', None, 'col'), parts along dimension 0, may hold values from -6 to 6
- kernel: float32 [3, 3, 3, 256, 256], P(None, None, None, None, 'col'), may hold values from -0.078125 to 0.078125
- bias: float32 [256], P('col'), may hold values from -1 to 1
Outputs:
- output: float32 [16, 32, 128, 256], P(('groups', 'gx'), 'gy', None, 'col'), parts along dimension 0
The draws below stay inside these ranges and needn't reach their ends.
There are 2 independent parts, one for each index of `groups`. The reference program is written for one: setup_inputs(seed, part) draws one part's arguments, and reference() takes and returns one part's arrays. A program takes and returns all parts, laid end to end along the dimension named above; an argument that names none is the same for every part. Nothing has to cross between parts.
All inputs are finite; a program needn't handle non-finite values.
Results may differ from the reference program's by a relative error of at most 0.000064.
Values sent between devices are 32-bit elements; how exact they have to be, the bound alone decides.
A program may use at most 64 MiB of HBM per device.

```python
import jax
import jax.numpy as jnp
from jax import lax

CI = 256
CO = 256
CZ = 128
NX = 8
NY = 32


def shard_levels(key, dims, shards, low, largest):
    def one(axis_at, parts):
        steps = jax.random.uniform(jax.random.fold_in(jax.random.fold_in(key, 6), axis_at), (parts,), jnp.float32, low / len(shards), largest / len(shards))
        return jnp.repeat(jnp.exp(steps), dims[axis_at] // parts).reshape((-1,) + (1,) * (len(dims) - axis_at - 1))

    gain = one(*shards[0])
    for cut in shards[1:]:
        gain = gain * one(*cut)
    return gain


def gaussian(key, dims, spread, reach, cuts=(), held_as=jnp.bfloat16):
    array = spread * jax.random.normal(key, dims, jnp.float32)
    if cuts:
        array = array * shard_levels(key, dims, cuts, -0.22, 0.18)
    return jnp.clip(array, -reach, reach).astype(held_as)


def setup_inputs(seed: int = 0, part: int = 0) -> dict:
    splits = jax.random.split(jax.random.key(seed), 4)
    own_keys = jax.random.split(jax.random.fold_in(splits[3], part), 4)
    return {
        "volume": gaussian(own_keys[0], (NX, NY, CZ, CI), 1.0, 6.0, ((0, 4), (1, 2), (3, 2)), jnp.float32),
        "kernel": gaussian(splits[1], (3, 3, 3, CI, CO), (27 * CI) ** -0.5, 0.078125, ((4, 2),), jnp.float32),
        "bias": jnp.clip(jax.random.uniform(splits[2], (CO,), jnp.float32, -1.0, 1.0) * shard_levels(splits[2], (CO,), ((0, 2),), -0.4, 0.0), -1.0, 1.0),
    }


def reference(volume, kernel, bias):
    result = lax.conv_general_dilated(volume[None], kernel, (1, 1, 1), "SAME", dimension_numbers=("NDHWC", "DHWIO", "NDHWC"), precision=lax.Precision.HIGHEST)[0]
    return result + bias
```

```python
import functools

import jax
import jax.numpy as jnp
from jax import lax
from jax.experimental import pallas as pl
from jax.experimental.pallas import tpu as pltpu
from jax.sharding import PartitionSpec as P

MESH = pl.DeviceIdType.MESH
R = 4


def split(x):
    high = x.astype(jnp.bfloat16)
    return high, (x - high.astype(jnp.float32)).astype(jnp.bfloat16)


def kernel(shape, v, w, bias, out, xin, hi, lo, w_raw, w_all, w_low, acc, loc, s_sib, r_sib, s_gx, r_gx, s_fw, r_fw, s_gy, r_gy, s_co, r_co, s_out):
    X, Y, Z, C = shape
    units = Y // R
    K = 3 * 2 * C
    col, gx, gy = lax.axis_index("col"), lax.axis_index("gx"), lax.axis_index("gy")
    nx, ny = lax.axis_size("gx"), lax.axis_size("gy")
    other = 1 - col
    has_x = (gx > 0, gx < nx - 1)
    to_x = (gx - 1, gx + 1)
    has_y = (gy > 0, gy < ny - 1)
    to_y = (gy - 1, gy + 1)
    layer_of = (0, X + 1)
    row_of = (0, Y + 1)

    own = pltpu.make_async_copy(v, xin.at[col, pl.ds(1, X), pl.ds(1, Y)], loc.at[0])
    weights = pltpu.make_async_copy(w, w_raw, loc.at[1])
    own.start()
    weights.start()

    barrier = pltpu.get_barrier_semaphore()

    def greet(device):
        pl.semaphore_signal(barrier, inc=1, device_id=device, device_id_type=MESH)

    greet({"col": other})
    count = jnp.int32(1)
    for side in range(2):
        @pl.when(has_x[side])
        def _():
            greet({"gx": to_x[side]})

        @pl.when(has_y[side])
        def _():
            greet({"gy": to_y[side]})
            greet({"gy": to_y[side], "col": other})

        count = count + has_x[side].astype(jnp.int32) + 2 * has_y[side].astype(jnp.int32)
    pl.semaphore_wait(barrier, count)

    def remote(src, dst, send, recv, device):
        return pltpu.make_async_remote_copy(src_ref=src, dst_ref=dst, send_sem=send, recv_sem=recv, device_id=device, device_id_type=MESH)

    sib_rows = [(R - 1, R + 2)]
    for u in range(2, units):
        sib_rows.append((u * R + 1, R if u < units - 1 else R - 1))
    sib_rows.append((0, R - 1))

    def sib(i, slot):
        start, size = sib_rows[i]
        return remote(v.at[:, pl.ds(start, size)], xin.at[slot, pl.ds(1, X), pl.ds(start + 1, size)], s_sib.at[i], r_sib.at[i], {"col": other})

    x_rows = [(0, 1), (Y - 1, 1)]
    for u in range(units):
        x_rows.append((u * R + 1, R if u < units - 1 else R - 2))

    def layer(side, i):
        start, size = x_rows[i]
        n = side * len(x_rows) + i
        return remote(v.at[0 if side == 0 else X - 1, pl.ds(start, size)], xin.at[col, layer_of[1 - side], pl.ds(start + 1, size)], s_gx.at[n], r_gx.at[n], {"gx": to_x[side]})

    def forward(side, i, slot):
        start, size = x_rows[i]
        n = side * len(x_rows) + i
        at = xin.at[slot, layer_of[side], pl.ds(start + 1, size)]
        return remote(at, at, s_fw.at[n], r_fw.at[n], {"col": other})

    def row(side, far, slot):
        n = side * 2 + far
        return remote(v.at[:, 0 if side == 0 else Y - 1], xin.at[slot, pl.ds(1, X), row_of[1 - side]], s_gy.at[n], r_gy.at[n],
                      {"gy": to_y[side], "col": other} if far else {"gy": to_y[side]})

    def corner(x_side, side, far, slot):
        n = (x_side * 2 + side) * 2 + far
        return remote(xin.at[col, layer_of[x_side], 1 if side == 0 else Y], xin.at[slot, layer_of[x_side], row_of[1 - side]], s_co.at[n], r_co.at[n],
                      {"gy": to_y[side], "col": other} if far else {"gy": to_y[side]})

    for i in range(len(x_rows)):
        for side in range(2):
            @pl.when(has_x[side])
            def _():
                layer(side, i).start()
        if i < len(sib_rows):
            sib(i, col).start()
        if i == 1:
            for side in range(2):
                @pl.when(has_y[side])
                def _():
                    row(side, 0, col).start()
                    row(side, 1, col).start()

    weights.wait()
    O = w.shape[-1]
    wide = 3 * O

    def prepare(t, _):
        at = pl.ds(pl.multiple_of(t * 2 * C, 2 * C), 2 * C)
        for c in range(3):
            high, low = split(w_raw[t, c])
            w_all[at, c * O:(c + 1) * O] = high
            w_all[at, wide + c * O:wide + (c + 1) * O] = low

            @pl.when(t >= 3)
            def _():
                w_low[pl.ds(pl.multiple_of((t - 3) * 2 * C, 2 * C), 2 * C), c * O:(c + 1) * O] = high

            @pl.when(t < 6)
            def _():
                w_low[at, wide + c * O:wide + (c + 1) * O] = high
        return 0

    lax.fori_loop(0, 9, prepare, 0)

    def convert(layers, start, size):
        def one(r, _):
            for l in layers:
                for slot in range(2):
                    high, low = split(xin[slot, l, start + r])
                    hi[l, start + r, :, slot * C:(slot + 1) * C] = high
                    lo[l, start + r, :, slot * C:(slot + 1) * C] = low
            return 0

        if size == 1:
            one(0, 0)
        else:
            lax.fori_loop(0, size, one, 0)

    def clear(layers, r):
        for l in layers:
            hi[l, r] = jnp.zeros((Z, 2 * C), jnp.bfloat16)
            lo[l, r] = jnp.zeros((Z, 2 * C), jnp.bfloat16)

    inner = tuple(range(1, X + 1))
    M = R * Z
    place = lax.broadcasted_iota(jnp.int32, (M, O), 0) % Z

    def rows(ref, layers, r0):
        return jnp.concatenate([ref[l, pl.ds(r0 + b, R)].reshape(M, 2 * C) for l in layers for b in range(3)], axis=1)

    def dot(x, y):
        return jnp.dot(x, y, preferred_element_type=jnp.float32)

    def joined(before, here, after):
        return (here + jnp.where(place == 0, 0.0, pltpu.roll(before, 1, 0)) + jnp.where(place == Z - 1, 0.0, pltpu.roll(after, M - 1, 0))).reshape(R, Z, O)

    def high_sums(x, first, depth):
        t = [dot(x, w_all[first:first + depth, n * 2 * O:(n + 1) * 2 * O]) for n in range(3)]
        return [t[0][:, :O] + t[1][:, O:], t[0][:, O:] + t[2][:, :O], t[1][:, :O] + t[2][:, O:]]

    def local_unit(r0):
        x = rows(lo, inner, r0)
        t = [dot(x, w_low[:, n * 2 * O:(n + 1) * 2 * O]) for n in range(3)]
        low = [[t[0][:, :O], t[0][:, O:], t[1][:, :O]], [t[1][:, O:], t[2][:, :O], t[2][:, O:]]]
        x = rows(hi, inner, r0)
        for o in range(2):
            s = high_sums(x, K if o == 0 else 0, 2 * K)
            acc[o, pl.ds(r0, R)] = joined(*[a + b for a, b in zip(s, low[o])]) + bias[...]

    def outer_unit(side, r0):
        first = 0 if side == 0 else 2 * K
        x = rows(lo, (layer_of[side],), r0)
        t = dot(x, w_all[first:first + K, :2 * O])
        low = [t[:, :O], t[:, O:], dot(x, w_all[first:first + K, 2 * O:wide])]
        s = high_sums(rows(hi, (layer_of[side],), r0), first, K)
        acc[side, pl.ds(r0, R)] += joined(*[a + b for a, b in zip(s, low)])

    def pass_on(i):
        for side in range(2):
            @pl.when(has_x[side])
            def _():
                layer(1 - side, i).wait_recv()
                forward(side, i, col).start()
                if i < 2:
                    @pl.when(has_y[i])
                    def _():
                        corner(side, i, 0, col).start()
                        corner(side, i, 1, col).start()

    def take_row(side):
        @pl.when(has_y[side])
        def _():
            row(1 - side, 0, col).wait_recv()
            row(1 - side, 1, other).wait_recv()
            convert(inner, row_of[side], 1)

        @pl.when(jnp.logical_not(has_y[side]))
        def _():
            clear(inner, row_of[side])

    def take_layer(i):
        for side in range(2):
            @pl.when(has_x[side])
            def _():
                forward(side, i, other).wait_recv()
                convert((layer_of[side],), x_rows[i][0] + 1, x_rows[i][1])
                if i < 2:
                    @pl.when(has_y[i])
                    def _():
                        corner(side, 1 - i, 0, col).wait_recv()
                        corner(side, 1 - i, 1, other).wait_recv()
                        convert((layer_of[side],), row_of[i], 1)

                    @pl.when(jnp.logical_not(has_y[i]))
                    def _():
                        clear((layer_of[side],), row_of[i])

    own.wait()

    def local_step(k, _):
        for kk in range(units):
            @pl.when(k == kk)
            def _():
                sib(kk, other).wait_recv()
                convert(inner, sib_rows[kk][0] + 1, sib_rows[kk][1])
                if kk == units - 2:
                    take_row(1)
                if kk == units - 1:
                    take_row(0)
        local_unit(lax.rem(k + 1, units) * R)
        for kk in range(units):
            @pl.when(k == kk)
            def _():
                if kk == 0:
                    pass_on(0)
                    pass_on(1)
                else:
                    pass_on(kk + 1)
        return 0

    lax.fori_loop(0, units, local_step, 0)

    def store(r0, n):
        return pltpu.make_async_copy(acc.at[:, pl.ds(r0, R)], out.at[:, pl.ds(r0, R)], s_out.at[n])

    def outer_step(k, _):
        for kk in range(units):
            @pl.when(k == kk)
            def _():
                if kk == 0:
                    take_layer(0)
                    take_layer(1)
                take_layer(kk + 2)
        for side in range(2):
            @pl.when(has_x[side])
            def _():
                outer_unit(side, k * R)
        store(k * R, k).start()

        @pl.when(k == 0)
        def _():
            pass_on(units + 1)
        return 0

    lax.fori_loop(0, units, outer_step, 0)

    for i in range(len(sib_rows)):
        sib(i, col).wait_send()
    for side in range(2):
        @pl.when(has_x[side])
        def _():
            for i in range(len(x_rows)):
                layer(side, i).wait_send()
                forward(side, i, col).wait_send()

        @pl.when(has_y[side])
        def _():
            row(side, 0, col).wait_send()
            row(side, 1, col).wait_send()

        for x_side in range(2):
            @pl.when(jnp.logical_and(has_x[x_side], has_y[side]))
            def _():
                corner(x_side, side, 0, col).wait_send()
                corner(x_side, side, 1, col).wait_send()
    for k in range(units):
        store(k * R, k).wait()


def per_device(volume, weights, bias):
    X, Y, Z, C = volume.shape
    O = weights.shape[4]
    units = Y // R
    pieces = units + 2
    dma = pltpu.SemaphoreType.DMA
    call = pl.pallas_call(
        functools.partial(kernel, volume.shape),
        out_shape=jax.ShapeDtypeStruct((X, Y, Z, O), jnp.float32),
        in_specs=[pl.BlockSpec(memory_space=pl.ANY), pl.BlockSpec(memory_space=pl.ANY), pl.BlockSpec(memory_space=pltpu.VMEM)],
        out_specs=pl.BlockSpec(memory_space=pl.ANY),
        scratch_shapes=[
            pltpu.VMEM((2, X + 2, Y + 2, Z, C), jnp.float32),
            pltpu.VMEM((X + 2, Y + 2, Z, 2 * C), jnp.bfloat16),
            pltpu.VMEM((X + 2, Y + 2, Z, 2 * C), jnp.bfloat16),
            pltpu.VMEM((9, 3, 2 * C, O), jnp.float32),
            pltpu.VMEM((18 * C, 6 * O), jnp.bfloat16),
            pltpu.VMEM((12 * C, 6 * O), jnp.bfloat16),
            pltpu.VMEM((X, Y, Z, O), jnp.float32),
            dma((2,)),
            dma((units,)), dma((units,)),
            dma((2 * pieces,)), dma((2 * pieces,)),
            dma((2 * pieces,)), dma((2 * pieces,)),
            dma((4,)), dma((4,)),
            dma((8,)), dma((8,)),
            dma((units,)),
        ],
        compiler_params=pltpu.CompilerParams(collective_id=0, has_side_effects=True, vmem_limit_bytes=58 * 1024 * 1024),
    )
    return call(volume, weights.reshape(9, 3, 2 * C, O), bias.reshape(1, O))


def solution(mesh):
    placed = (P(("groups", "gx"), "gy", None, "col"), P(None, None, None, None, "col"), P("col"))
    return jax.shard_map(
        per_device,
        mesh=mesh,
        in_specs=placed,
        out_specs=P(("groups", "gx"), "gy", None, "col"),
        check_vma=False,
    )
```

```python
import functools

import jax
import jax.numpy as jnp
from jax import lax
from jax.experimental import pallas as pl
from jax.experimental.pallas import tpu as pltpu
from jax.sharding import PartitionSpec as P

MESH = pl.DeviceIdType.MESH
R = 4


def split(x):
    high = x.astype(jnp.bfloat16)
    return high, (x - high.astype(jnp.float32)).astype(jnp.bfloat16)


def kernel(shape, v, w, bias, out, xin, hi, lo, w_raw, w_all, w_low, acc, loc, s_sib, r_sib, s_gx, r_gx, s_fw, r_fw, s_gy, r_gy, s_co, r_co, s_out):
    X, Y, Z, C = shape
    units = Y // R
    K = 3 * 2 * C
    col, gx, gy = lax.axis_index("col"), lax.axis_index("gx"), lax.axis_index("gy")
    nx, ny = lax.axis_size("gx"), lax.axis_size("gy")
    other = 1 - col
    has_x = (gx > 0, gx < nx - 1)
    to_x = (gx - 1, gx + 1)
    has_y = (gy > 0, gy < ny - 1)
    to_y = (gy - 1, gy + 1)
    layer_of = (0, X + 1)
    row_of = (0, Y + 1)

    own = pltpu.make_async_copy(v, xin.at[col, pl.ds(1, X), pl.ds(1, Y)], loc.at[0])
    weights = [pltpu.make_async_copy(w.at[pl.ds(3 * a, 3)], w_raw.at[pl.ds(3 * a, 3)], loc.at[1 + a]) for a in range(3)]
    for a in range(3):
        weights[a].start()
    own.start()

    barrier = pltpu.get_barrier_semaphore()

    def greet(device):
        pl.semaphore_signal(barrier, inc=1, device_id=device, device_id_type=MESH)

    greet({"col": other})
    count = jnp.int32(1)
    for side in range(2):
        @pl.when(has_x[side])
        def _():
            greet({"gx": to_x[side]})

        @pl.when(has_y[side])
        def _():
            greet({"gy": to_y[side]})
            greet({"gy": to_y[side], "col": other})

        count = count + has_x[side].astype(jnp.int32) + 2 * has_y[side].astype(jnp.int32)
    pl.semaphore_wait(barrier, count)

    def remote(src, dst, send, recv, device):
        return pltpu.make_async_remote_copy(src_ref=src, dst_ref=dst, send_sem=send, recv_sem=recv, device_id=device, device_id_type=MESH)

    sib_rows = [(R - 1, R + 2)]
    for u in range(2, units):
        sib_rows.append((u * R + 1, R if u < units - 1 else R - 1))
    sib_rows.append((0, R - 1))

    def sib(i, slot):
        start, size = sib_rows[i]
        return remote(v.at[:, pl.ds(start, size)], xin.at[slot, pl.ds(1, X), pl.ds(start + 1, size)], s_sib.at[i], r_sib.at[i], {"col": other})

    x_rows = [(0, 1), (Y - 1, 1)]
    for u in range(units):
        x_rows.append((u * R + 1, R if u < units - 1 else R - 2))

    def layer(side, i):
        start, size = x_rows[i]
        n = side * len(x_rows) + i
        return remote(v.at[0 if side == 0 else X - 1, pl.ds(start, size)], xin.at[col, layer_of[1 - side], pl.ds(start + 1, size)], s_gx.at[n], r_gx.at[n], {"gx": to_x[side]})

    def forward(side, i, slot):
        start, size = x_rows[i]
        n = side * len(x_rows) + i
        at = xin.at[slot, layer_of[side], pl.ds(start + 1, size)]
        return remote(at, at, s_fw.at[n], r_fw.at[n], {"col": other})

    def row(side, far, slot):
        n = side * 2 + far
        return remote(v.at[:, 0 if side == 0 else Y - 1], xin.at[slot, pl.ds(1, X), row_of[1 - side]], s_gy.at[n], r_gy.at[n],
                      {"gy": to_y[side], "col": other} if far else {"gy": to_y[side]})

    def corner(x_side, side, far, slot):
        n = (x_side * 2 + side) * 2 + far
        return remote(xin.at[col, layer_of[x_side], 1 if side == 0 else Y], xin.at[slot, layer_of[x_side], row_of[1 - side]], s_co.at[n], r_co.at[n],
                      {"gy": to_y[side], "col": other} if far else {"gy": to_y[side]})

    for i in range(len(x_rows)):
        for side in range(2):
            @pl.when(has_x[side])
            def _():
                layer(side, i).start()
        if i < len(sib_rows):
            sib(i, col).start()
        if i == 1:
            for side in range(2):
                @pl.when(has_y[side])
                def _():
                    row(side, 0, col).start()
                    row(side, 1, col).start()

    O = w.shape[-1]
    wide = 3 * O

    def prepare(t, _):
        at = pl.ds(pl.multiple_of(t * 2 * C, 2 * C), 2 * C)
        for c in range(3):
            high, low = split(w_raw[t, c])
            w_all[at, c * O:(c + 1) * O] = high
            w_all[at, wide + c * O:wide + (c + 1) * O] = low

            @pl.when(t >= 3)
            def _():
                w_low[pl.ds(pl.multiple_of((t - 3) * 2 * C, 2 * C), 2 * C), c * O:(c + 1) * O] = high

            @pl.when(t < 6)
            def _():
                w_low[at, wide + c * O:wide + (c + 1) * O] = high
        return 0

    for a in range(3):
        weights[a].wait()
        lax.fori_loop(3 * a, 3 * a + 3, prepare, 0)

    def convert(layers, start, size):
        def one(r, _):
            for l in layers:
                for slot in range(2):
                    high, low = split(xin[slot, l, start + r])
                    hi[l, start + r, :, slot * C:(slot + 1) * C] = high
                    lo[l, start + r, :, slot * C:(slot + 1) * C] = low
            return 0

        if size == 1:
            one(0, 0)
        else:
            lax.fori_loop(0, size, one, 0)

    def clear(layers, r):
        for l in layers:
            hi[l, r] = jnp.zeros((Z, 2 * C), jnp.bfloat16)
            lo[l, r] = jnp.zeros((Z, 2 * C), jnp.bfloat16)

    inner = tuple(range(1, X + 1))
    M = R * Z
    place = lax.broadcasted_iota(jnp.int32, (M, O), 0) % Z

    def rows(ref, layers, r0):
        return jnp.concatenate([ref[l, pl.ds(r0 + b, R)].reshape(M, 2 * C) for l in layers for b in range(3)], axis=1)

    def dot(x, y):
        return jnp.dot(x, y, preferred_element_type=jnp.float32)

    def joined(before, here, after):
        return (here + jnp.where(place == 0, 0.0, pltpu.roll(before, 1, 0)) + jnp.where(place == Z - 1, 0.0, pltpu.roll(after, M - 1, 0))).reshape(R, Z, O)

    def high_sums(x, first, depth):
        t = [dot(x, w_all[first:first + depth, n * 2 * O:(n + 1) * 2 * O]) for n in range(3)]
        return [t[0][:, :O] + t[1][:, O:], t[0][:, O:] + t[2][:, :O], t[1][:, :O] + t[2][:, O:]]

    def local_unit(r0):
        x = rows(lo, inner, r0)
        t = [dot(x, w_low[:, n * 2 * O:(n + 1) * 2 * O]) for n in range(3)]
        low = [[t[0][:, :O], t[0][:, O:], t[1][:, :O]], [t[1][:, O:], t[2][:, :O], t[2][:, O:]]]
        x = rows(hi, inner, r0)
        for o in range(2):
            s = high_sums(x, K if o == 0 else 0, 2 * K)
            acc[o, pl.ds(r0, R)] = joined(*[a + b for a, b in zip(s, low[o])]) + bias[...]

    def outer_unit(side, r0):
        first = 0 if side == 0 else 2 * K
        x = rows(lo, (layer_of[side],), r0)
        t = dot(x, w_all[first:first + K, :2 * O])
        low = [t[:, :O], t[:, O:], dot(x, w_all[first:first + K, 2 * O:wide])]
        s = high_sums(rows(hi, (layer_of[side],), r0), first, K)
        acc[side, pl.ds(r0, R)] += joined(*[a + b for a, b in zip(s, low)])

    def pass_on(i):
        for side in range(2):
            @pl.when(has_x[side])
            def _():
                layer(1 - side, i).wait_recv()
                forward(side, i, col).start()
                if i < 2:
                    @pl.when(has_y[i])
                    def _():
                        corner(side, i, 0, col).start()
                        corner(side, i, 1, col).start()

    def take_row(side):
        @pl.when(has_y[side])
        def _():
            row(1 - side, 0, col).wait_recv()
            row(1 - side, 1, other).wait_recv()
            convert(inner, row_of[side], 1)

        @pl.when(jnp.logical_not(has_y[side]))
        def _():
            clear(inner, row_of[side])

    def take_layer(i):
        for side in range(2):
            @pl.when(has_x[side])
            def _():
                forward(side, i, other).wait_recv()
                convert((layer_of[side],), x_rows[i][0] + 1, x_rows[i][1])
                if i < 2:
                    @pl.when(has_y[i])
                    def _():
                        corner(side, 1 - i, 0, col).wait_recv()
                        corner(side, 1 - i, 1, other).wait_recv()
                        convert((layer_of[side],), row_of[i], 1)

                    @pl.when(jnp.logical_not(has_y[i]))
                    def _():
                        clear((layer_of[side],), row_of[i])

    own.wait()

    def local_step(k, _):
        for kk in range(units):
            @pl.when(k == kk)
            def _():
                sib(kk, other).wait_recv()
                convert(inner, sib_rows[kk][0] + 1, sib_rows[kk][1])
                if kk == units - 2:
                    take_row(1)
                if kk == units - 1:
                    take_row(0)
        local_unit(lax.rem(k + 1, units) * R)
        for kk in range(units):
            @pl.when(k == kk)
            def _():
                if kk == 1:
                    pass_on(0)
                    pass_on(1)
                elif kk > 1:
                    pass_on(kk)
        return 0

    lax.fori_loop(0, units, local_step, 0)

    def store(r0, n):
        return pltpu.make_async_copy(acc.at[:, pl.ds(r0, R)], out.at[:, pl.ds(r0, R)], s_out.at[n])

    def outer_step(k, _):
        for kk in range(units):
            @pl.when(k == kk)
            def _():
                if kk == 0:
                    take_layer(0)
                    take_layer(1)
                take_layer(kk + 2)
        for side in range(2):
            @pl.when(has_x[side])
            def _():
                outer_unit(side, k * R)
        store(k * R, k).start()

        for kk in range(2):
            @pl.when(k == kk)
            def _():
                pass_on(units + kk)
        return 0

    lax.fori_loop(0, units, outer_step, 0)

    for i in range(len(sib_rows)):
        sib(i, col).wait_send()
    for side in range(2):
        @pl.when(has_x[side])
        def _():
            for i in range(len(x_rows)):
                layer(side, i).wait_send()
                forward(side, i, col).wait_send()

        @pl.when(has_y[side])
        def _():
            row(side, 0, col).wait_send()
            row(side, 1, col).wait_send()

        for x_side in range(2):
            @pl.when(jnp.logical_and(has_x[x_side], has_y[side]))
            def _():
                corner(x_side, side, 0, col).wait_send()
                corner(x_side, side, 1, col).wait_send()
    for k in range(units):
        store(k * R, k).wait()


def per_device(volume, weights, bias):
    X, Y, Z, C = volume.shape
    O = weights.shape[4]
    units = Y // R
    pieces = units + 2
    dma = pltpu.SemaphoreType.DMA
    call = pl.pallas_call(
        functools.partial(kernel, volume.shape),
        out_shape=jax.ShapeDtypeStruct((X, Y, Z, O), jnp.float32),
        in_specs=[pl.BlockSpec(memory_space=pltpu.HBM), pl.BlockSpec(memory_space=pltpu.HBM), pl.BlockSpec(memory_space=pltpu.VMEM)],
        out_specs=pl.BlockSpec(memory_space=pl.ANY),
        scratch_shapes=[
            pltpu.VMEM((2, X + 2, Y + 2, Z, C), jnp.float32),
            pltpu.VMEM((X + 2, Y + 2, Z, 2 * C), jnp.bfloat16),
            pltpu.VMEM((X + 2, Y + 2, Z, 2 * C), jnp.bfloat16),
            pltpu.VMEM((9, 3, 2 * C, O), jnp.float32),
            pltpu.VMEM((18 * C, 6 * O), jnp.bfloat16),
            pltpu.VMEM((12 * C, 6 * O), jnp.bfloat16),
            pltpu.VMEM((X, Y, Z, O), jnp.float32),
            dma((4,)),
            dma((units,)), dma((units,)),
            dma((2 * pieces,)), dma((2 * pieces,)),
            dma((2 * pieces,)), dma((2 * pieces,)),
            dma((4,)), dma((4,)),
            dma((8,)), dma((8,)),
            dma((units,)),
        ],
        compiler_params=pltpu.CompilerParams(collective_id=0, has_side_effects=True, vmem_limit_bytes=51 * 1024 * 1024),
    )
    return call(volume, weights.reshape(9, 3, 2 * C, O), bias.reshape(1, O))


def solution(mesh):
    placed = (P(("groups", "gx"), "gy", None, "col"), P(None, None, None, None, "col"), P("col"))
    return jax.shard_map(
        per_device,
        mesh=mesh,
        in_specs=placed,
        out_specs=P(("groups", "gx"), "gy", None, "col"),
        check_vma=False,
    )
```

```python
import functools

import jax
import jax.numpy as jnp
from jax import lax
from jax.experimental import pallas as pl
from jax.experimental.pallas import tpu as pltpu
from jax.sharding import PartitionSpec as P

MESH = pl.DeviceIdType.MESH
R = 4


def split(x):
    high = x.astype(jnp.bfloat16)
    return high, (x - high.astype(jnp.float32)).astype(jnp.bfloat16)


def kernel(shape, v, w, bias, out, xin, hi, lo, w_raw, w_all, w_low, loc, s_sib, r_sib, s_gx, r_gx, s_fw, r_fw, s_gy, r_gy, s_co, r_co, s_out):
    X, Y, Z, C = shape
    acc = out
    units = Y // R
    K = 3 * 2 * C
    col, gx, gy = lax.axis_index("col"), lax.axis_index("gx"), lax.axis_index("gy")
    nx, ny = lax.axis_size("gx"), lax.axis_size("gy")
    other = 1 - col
    has_x = (gx > 0, gx < nx - 1)
    to_x = (gx - 1, gx + 1)
    has_y = (gy > 0, gy < ny - 1)
    to_y = (gy - 1, gy + 1)
    layer_of = (0, X + 1)
    row_of = (0, Y + 1)

    own = pltpu.make_async_copy(v, xin.at[col, pl.ds(1, X), pl.ds(1, Y)], loc.at[0])
    weights = [pltpu.make_async_copy(w.at[pl.ds(3 * a, 3)], w_raw.at[pl.ds(3 * a, 3)], loc.at[1 + a]) for a in range(3)]
    for a in range(3):
        weights[a].start()
    own.start()

    barrier = pltpu.get_barrier_semaphore()

    def greet(device):
        pl.semaphore_signal(barrier, inc=1, device_id=device, device_id_type=MESH)

    greet({"col": other})
    count = jnp.int32(1)
    for side in range(2):
        @pl.when(has_x[side])
        def _():
            greet({"gx": to_x[side]})

        @pl.when(has_y[side])
        def _():
            greet({"gy": to_y[side]})
            greet({"gy": to_y[side], "col": other})

        count = count + has_x[side].astype(jnp.int32) + 2 * has_y[side].astype(jnp.int32)
    pl.semaphore_wait(barrier, count)

    def remote(src, dst, send, recv, device):
        return pltpu.make_async_remote_copy(src_ref=src, dst_ref=dst, send_sem=send, recv_sem=recv, device_id=device, device_id_type=MESH)

    sib_rows = [(R - 1, R + 2)]
    for u in range(2, units):
        sib_rows.append((u * R + 1, R if u < units - 1 else R - 1))
    sib_rows.append((0, R - 1))

    def sib(i, slot):
        start, size = sib_rows[i]
        return remote(v.at[:, pl.ds(start, size)], xin.at[slot, pl.ds(1, X), pl.ds(start + 1, size)], s_sib.at[i], r_sib.at[i], {"col": other})

    x_rows = [(0, 1), (Y - 1, 1)]
    for u in range(units):
        x_rows.append((u * R + 1, R if u < units - 1 else R - 2))

    def layer(side, i):
        start, size = x_rows[i]
        n = side * len(x_rows) + i
        return remote(v.at[0 if side == 0 else X - 1, pl.ds(start, size)], xin.at[col, layer_of[1 - side], pl.ds(start + 1, size)], s_gx.at[n], r_gx.at[n], {"gx": to_x[side]})

    def forward(side, i, slot):
        start, size = x_rows[i]
        n = side * len(x_rows) + i
        at = xin.at[slot, layer_of[side], pl.ds(start + 1, size)]
        return remote(at, at, s_fw.at[n], r_fw.at[n], {"col": other})

    def row(side, far, slot):
        n = side * 2 + far
        return remote(v.at[:, 0 if side == 0 else Y - 1], xin.at[slot, pl.ds(1, X), row_of[1 - side]], s_gy.at[n], r_gy.at[n],
                      {"gy": to_y[side], "col": other} if far else {"gy": to_y[side]})

    def corner(x_side, side, far, slot):
        n = (x_side * 2 + side) * 2 + far
        return remote(xin.at[col, layer_of[x_side], 1 if side == 0 else Y], xin.at[slot, layer_of[x_side], row_of[1 - side]], s_co.at[n], r_co.at[n],
                      {"gy": to_y[side], "col": other} if far else {"gy": to_y[side]})

    for i in range(len(x_rows)):
        for side in range(2):
            @pl.when(has_x[side])
            def _():
                layer(side, i).start()
        if i < len(sib_rows):
            sib(i, col).start()
        if i == 1:
            for side in range(2):
                @pl.when(has_y[side])
                def _():
                    row(side, 0, col).start()
                    row(side, 1, col).start()

    O = w.shape[-1]
    wide = 3 * O

    def prepare(t, _):
        at = pl.ds(pl.multiple_of(t * 2 * C, 2 * C), 2 * C)
        for c in range(3):
            high, low = split(w_raw[t, c])
            w_all[at, c * O:(c + 1) * O] = high
            w_all[at, wide + c * O:wide + (c + 1) * O] = low

            @pl.when(t >= 3)
            def _():
                w_low[pl.ds(pl.multiple_of((t - 3) * 2 * C, 2 * C), 2 * C), c * O:(c + 1) * O] = high

            @pl.when(t < 6)
            def _():
                w_low[at, wide + c * O:wide + (c + 1) * O] = high
        return 0

    for a in range(3):
        weights[a].wait()
        lax.fori_loop(3 * a, 3 * a + 3, prepare, 0)

    def convert(layers, start, size):
        def one(r, _):
            for l in layers:
                for slot in range(2):
                    high, low = split(xin[slot, l, start + r])
                    hi[l, start + r, :, slot * C:(slot + 1) * C] = high
                    lo[l, start + r, :, slot * C:(slot + 1) * C] = low
            return 0

        if size == 1:
            one(0, 0)
        else:
            lax.fori_loop(0, size, one, 0)

    def clear(layers, r):
        for l in layers:
            hi[l, r] = jnp.zeros((Z, 2 * C), jnp.bfloat16)
            lo[l, r] = jnp.zeros((Z, 2 * C), jnp.bfloat16)

    inner = tuple(range(1, X + 1))
    M = R * Z
    place = lax.broadcasted_iota(jnp.int32, (M, O), 0) % Z

    def rows(ref, layers, r0):
        return jnp.concatenate([ref[l, pl.ds(r0 + b, R)].reshape(M, 2 * C) for l in layers for b in range(3)], axis=1)

    def dot(x, y):
        return jnp.dot(x, y, preferred_element_type=jnp.float32)

    def joined(before, here, after):
        return (here + jnp.where(place == 0, 0.0, pltpu.roll(before, 1, 0)) + jnp.where(place == Z - 1, 0.0, pltpu.roll(after, M - 1, 0))).reshape(R, Z, O)

    def high_sums(x, first, depth):
        t = [dot(x, w_all[first:first + depth, n * 2 * O:(n + 1) * 2 * O]) for n in range(3)]
        return [t[0][:, :O] + t[1][:, O:], t[0][:, O:] + t[2][:, :O], t[1][:, :O] + t[2][:, O:]]

    def local_unit(r0):
        x = rows(lo, inner, r0)
        t = [dot(x, w_low[:, n * 2 * O:(n + 1) * 2 * O]) for n in range(3)]
        low = [[t[0][:, :O], t[0][:, O:], t[1][:, :O]], [t[1][:, O:], t[2][:, :O], t[2][:, O:]]]
        x = rows(hi, inner, r0)
        for o in range(2):
            s = high_sums(x, K if o == 0 else 0, 2 * K)
            acc[o, pl.ds(r0, R)] = joined(*[a + b for a, b in zip(s, low[o])]) + bias[...]

    def outer_unit(side, r0):
        first = 0 if side == 0 else 2 * K
        x = rows(lo, (layer_of[side],), r0)
        t = dot(x, w_all[first:first + K, :2 * O])
        low = [t[:, :O], t[:, O:], dot(x, w_all[first:first + K, 2 * O:wide])]
        s = high_sums(rows(hi, (layer_of[side],), r0), first, K)
        acc[side, pl.ds(r0, R)] += joined(*[a + b for a, b in zip(s, low)])

    def pass_on(i):
        for side in range(2):
            @pl.when(has_x[side])
            def _():
                layer(1 - side, i).wait_recv()
                forward(side, i, col).start()
                if i < 2:
                    @pl.when(has_y[i])
                    def _():
                        corner(side, i, 0, col).start()
                        corner(side, i, 1, col).start()

    def take_row(side):
        @pl.when(has_y[side])
        def _():
            row(1 - side, 0, col).wait_recv()
            row(1 - side, 1, other).wait_recv()
            convert(inner, row_of[side], 1)

        @pl.when(jnp.logical_not(has_y[side]))
        def _():
            clear(inner, row_of[side])

    def take_layer(i):
        for side in range(2):
            @pl.when(has_x[side])
            def _():
                forward(side, i, other).wait_recv()
                convert((layer_of[side],), x_rows[i][0] + 1, x_rows[i][1])
                if i < 2:
                    @pl.when(has_y[i])
                    def _():
                        corner(side, 1 - i, 0, col).wait_recv()
                        corner(side, 1 - i, 1, other).wait_recv()
                        convert((layer_of[side],), row_of[i], 1)

                    @pl.when(jnp.logical_not(has_y[i]))
                    def _():
                        clear((layer_of[side],), row_of[i])

    own.wait()

    def local_step(k, _):
        for kk in range(units):
            @pl.when(k == kk)
            def _():
                sib(kk, other).wait_recv()
                convert(inner, sib_rows[kk][0] + 1, sib_rows[kk][1])
                if kk == units - 2:
                    take_row(1)
                if kk == units - 1:
                    take_row(0)
        local_unit(lax.rem(k + 1, units) * R)
        for kk in range(units):
            @pl.when(k == kk)
            def _():
                if kk == 1:
                    pass_on(0)
                    pass_on(1)
                elif kk > 1:
                    pass_on(kk)
        return 0

    lax.fori_loop(0, units, local_step, 0)

    def store(r0, n):
        return pltpu.make_async_copy(acc.at[:, pl.ds(r0, R)], out.at[:, pl.ds(r0, R)], s_out.at[n])

    def outer_step(k, _):
        for kk in range(units):
            @pl.when(k == kk)
            def _():
                if kk == 0:
                    take_layer(0)
                    take_layer(1)
                take_layer(kk + 2)
        both = jnp.logical_and(has_x[0], has_x[1])

        @pl.when(both)
        def _():
            outer_unit(0, k * R)
            outer_unit(1, k * R)

        for side in range(2):
            @pl.when(jnp.logical_and(has_x[side], jnp.logical_not(both)))
            def _():
                outer_unit(side, k * R)

        for kk in range(2):
            @pl.when(k == kk)
            def _():
                pass_on(units + kk)
        return 0

    lax.fori_loop(0, units, outer_step, 0)

    for i in range(len(sib_rows)):
        sib(i, col).wait_send()
    for side in range(2):
        @pl.when(has_x[side])
        def _():
            for i in range(len(x_rows)):
                layer(side, i).wait_send()
                forward(side, i, col).wait_send()

        @pl.when(has_y[side])
        def _():
            row(side, 0, col).wait_send()
            row(side, 1, col).wait_send()

        for x_side in range(2):
            @pl.when(jnp.logical_and(has_x[x_side], has_y[side]))
            def _():
                corner(x_side, side, 0, col).wait_send()
                corner(x_side, side, 1, col).wait_send()


def per_device(volume, weights, bias):
    X, Y, Z, C = volume.shape
    O = weights.shape[4]
    units = Y // R
    pieces = units + 2
    dma = pltpu.SemaphoreType.DMA
    call = pl.pallas_call(
        functools.partial(kernel, volume.shape),
        out_shape=jax.ShapeDtypeStruct((X, Y, Z, O), jnp.float32),
        in_specs=[pl.BlockSpec(memory_space=pltpu.HBM), pl.BlockSpec(memory_space=pltpu.HBM), pl.BlockSpec(memory_space=pltpu.VMEM)],
        out_specs=pl.BlockSpec(memory_space=pltpu.VMEM),
        scratch_shapes=[
            pltpu.VMEM((2, X + 2, Y + 2, Z, C), jnp.float32),
            pltpu.VMEM((X + 2, Y + 2, Z, 2 * C), jnp.bfloat16),
            pltpu.VMEM((X + 2, Y + 2, Z, 2 * C), jnp.bfloat16),
            pltpu.VMEM((9, 3, 2 * C, O), jnp.float32),
            pltpu.VMEM((18 * C, 6 * O), jnp.bfloat16),
            pltpu.VMEM((12 * C, 6 * O), jnp.bfloat16),
            dma((4,)),
            dma((units,)), dma((units,)),
            dma((2 * pieces,)), dma((2 * pieces,)),
            dma((2 * pieces,)), dma((2 * pieces,)),
            dma((4,)), dma((4,)),
            dma((8,)), dma((8,)),
            dma((units,)),
        ],
        compiler_params=pltpu.CompilerParams(collective_id=0, has_side_effects=True, vmem_limit_bytes=51 * 1024 * 1024),
    )
    return call(volume, weights.reshape(9, 3, 2 * C, O), bias.reshape(1, O))


def solution(mesh):
    placed = (P(("groups", "gx"), "gy", None, "col"), P(None, None, None, None, "col"), P("col"))
    return jax.shard_map(
        per_device,
        mesh=mesh,
        in_specs=placed,
        out_specs=P(("groups", "gx"), "gy", None, "col"),
        check_vma=False,
    )
```
